32 devices in a mesh: cube: 4 (over y, x), grid: 8 (over z, core).
Axes of the slice: x: 2, y: 2, z: 4, core: 2. Of those that a mesh axis runs over, the one named last changes fastest.
Arguments:
- parent_front: float32 [8192, 4, 4096], P('grid', 'cube'), as said below
- child_block: bfloat16 [4, 6144, 6144], P('cube', 'grid'), as said below
- child_panel: bfloat16 [4, 6144, 512], P('cube', 'grid'), may hold values from -0.15625 to 0.15625
- row_map: int32 [4, 6144], replicated, may hold values from 0 to 8191, as said below
Outputs:
- schur_block: float32 [8192, 4, 4096], P('grid', 'cube')
- panel_factor: float32 [8192, 4, 256], P('grid', 'cube')
The draws below stay inside these ranges and needn't reach their ends.
Inputs may be any that keep to these rules, and one draw needn't show every extreme that they name: Each row of row_map lists 6144 distinct parent rows. Cut the 6144 entries of a row into 768 entries for each grid index, and the parent rows into blocks of 1024: from one grid index at most 192 entries fall into one block, a number reached in every draw. `parent_front`: symmetric with a dominant positive diagonal. `child_block`: symmetric with a dominant positive diagonal.
All inputs are finite; a program needn't handle non-finite values.
Results may differ from the reference program's by a relative error of at most 0.0015.
Values may be sent and summed in bfloat16 or wider, within the bound.
A program may use at most 192 MiB of HBM per device.

```python
import jax
import jax.numpy as jnp
from jax import lax

PF = 8192
CB = 6144
PW = 512
N_GRID = 8


def symmetric_matrix(key, order, spread, diag_low, diag_high):
    first_key, second_key = jax.random.split(key)
    entries = jax.random.normal(first_key, (order, order), jnp.float32)
    entries = (entries + entries.T) * (spread * 0.7071)
    diagonal = jax.random.uniform(second_key, (order,), jnp.float32, diag_low, diag_high)
    return entries + jnp.diag(diagonal)


def draw_parent_front(key, part):
    fronts = [symmetric_matrix(jax.random.fold_in(key, 11 + parent_index), PF, 0.02, 3.0, 6.0) for parent_index in range(2)]
    stacked = jnp.stack(fronts)
    return stacked.reshape(2, PF, PF // 2, 2).transpose(1, 0, 3, 2).reshape(PF, 4, PF // 2)


def draw_child_block(key, part):
    blocks = [symmetric_matrix(jax.random.fold_in(key, 21 + child_index), CB, 0.01, 1.0, 2.0) for child_index in range(4)]
    return jnp.stack(blocks).astype(jnp.bfloat16)


def child_map(key):
    owners = N_GRID
    source_rows = CB // owners
    owned_rows = PF // owners
    mean_count = source_rows // owners
    first_key, second_key, third_key = jax.random.split(key, 3)
    order_draw = jax.random.permutation(first_key, owners).astype(jnp.int32)
    levels = jnp.where(order_draw < owners // 4, 2 * mean_count, jnp.where(order_draw < 3 * owners // 4, mean_count, 0)).astype(jnp.int32)
    source_ids = jnp.arange(owners, dtype=jnp.int32)[:, None]
    owner_ids = jnp.arange(owners, dtype=jnp.int32)[None, :]
    counts = levels[(owner_ids - source_ids) % owners]
    segment_end = jnp.cumsum(counts, axis=1)
    segment_start = segment_end - counts
    base_offset = jnp.cumsum(counts, axis=0) - counts
    positions = jnp.arange(source_rows, dtype=jnp.int32)
    owner_of = jnp.sum((positions[None, :, None] >= segment_end[:, None, :]).astype(jnp.int32), axis=2)
    start_sel = jnp.take_along_axis(segment_start, owner_of, axis=1)
    base_sel = jnp.take_along_axis(base_offset, owner_of, axis=1)
    offsets = base_sel + positions[None, :] - start_sel
    slot_tables = jax.vmap(lambda sub_key: jax.random.permutation(sub_key, owned_rows))(jax.random.split(second_key, owners)).astype(jnp.int32)
    slots = slot_tables[owner_of, offsets]
    parent_rows = owner_of * owned_rows + slots
    row_orders = jax.vmap(lambda sub_key: jax.random.permutation(sub_key, source_rows))(jax.random.split(third_key, owners)).astype(jnp.int32)
    child_rows = source_ids * source_rows + row_orders
    return jnp.zeros((CB,), jnp.int32).at[child_rows.reshape(-1)].set(parent_rows.reshape(-1).astype(jnp.int32))


def draw_row_map(key, part):
    return jnp.stack([child_map(jax.random.fold_in(key, 31 + child_index)) for child_index in range(4)])


def steps_of(stream_key, dims, pieces, least, top_value):
    gain, own = 1.0, jax.random.fold_in(stream_key, 6)
    for position, shards_of in pieces:
        draws = jnp.exp(jax.random.uniform(jax.random.fold_in(own, position), (shards_of,), jnp.float32, least / len(pieces), top_value / len(pieces)))
        gain = gain * jnp.repeat(draws, dims[position] // shards_of).reshape([-1 if axis == position else 1 for axis in range(len(dims))])
    return gain


def bell_draw(rng, dims, scale, reach, cuts=(), kind=jnp.bfloat16):
    values = scale * jax.random.normal(rng, dims, jnp.float32)
    if cuts:
        values = values * steps_of(rng, dims, cuts, -0.22, 0.18)
    return jnp.clip(values, -reach, reach).astype(kind)


def setup_inputs(seed: int = 0) -> dict:
    streams_of = jax.random.split(jax.random.key(seed), 5)
    return {
        "parent_front": draw_parent_front(jax.random.fold_in(streams_of[4], 71), 0),
        "child_block": draw_child_block(jax.random.fold_in(streams_of[4], 71), 0),
        "child_panel": bell_draw(streams_of[2], (4, CB, PW), (PW * 25 // 9) ** -0.5, 0.15625, ((0, 4), (1, 8))),
        "row_map": draw_row_map(jax.random.fold_in(streams_of[4], 71), 0),
    }


def contribution(block_data, panel_data):
    product = jnp.dot(panel_data.astype(jnp.float32), panel_data.T.astype(jnp.float32), preferred_element_type=jnp.float32)
    return (block_data.astype(jnp.float32) - product).astype(jnp.bfloat16)

def reference(parent_front, child_block, child_panel, row_map):
    schur_parts = []
    panel_parts = []
    for parent_index in range(2):
        front_matrix = jnp.stack([parent_front[:, 2 * parent_index, :], parent_front[:, 2 * parent_index + 1, :]], axis=2).reshape(PF, PF)
        for child_index in (2 * parent_index, 2 * parent_index + 1):
            update = contribution(child_block[child_index], child_panel[child_index]).astype(jnp.float32)
            indices = row_map[child_index]
            front_matrix = front_matrix.at[indices[:, None], indices[None, :]].add(update)
        lower_factor = jnp.linalg.cholesky(front_matrix[:PW, :PW])
        factor = lax.linalg.triangular_solve(lower_factor, front_matrix[:, :PW], left_side=False, lower=True, transpose_a=True)
        outer_term = jnp.dot(factor.astype(jnp.float32), factor.T.astype(jnp.float32), precision=lax.Precision.HIGHEST, preferred_element_type=jnp.float32)
        schur_matrix = front_matrix - outer_term
        schur_parts.append(schur_matrix.reshape(PF, PF // 2, 2).transpose(0, 2, 1))
        panel_parts.append(factor.reshape(PF, PW // 2, 2).transpose(0, 2, 1))
    return (jnp.concatenate(schur_parts, axis=1), jnp.concatenate(panel_parts, axis=1))
```

```python
import functools

import jax
import jax.numpy as jnp
from jax import lax
from jax.experimental import pallas as pl
from jax.experimental.pallas import tpu as pltpu
from jax.sharding import PartitionSpec as P

PW = 512
CHUNKS = 4
HIGHEST = lax.Precision.HIGHEST
NT = (((1,), (1,)), ((), ()))
VMEM_LIMIT = 56 * 1024 * 1024


def swapped(block, axis, distance):
    count = lax.axis_size(axis)
    route = []
    for low in range(count):
        high = low | 1 << distance
        if high != low and high < count:
            route += [(low, high), (high, low)]
    return lax.ppermute(block, axis, route)


def one_hot_tile(targets, sources):
    return jnp.where(targets == sources, 1.0, 0.0).astype(jnp.bfloat16)


def spread_kernel(depth, target_ref, map_ref, slab_ref, out_ref):
    total = None
    for step in range(map_ref.shape[0]):
        hot = one_hot_tile(target_ref[...], map_ref[step])
        part = lax.dot_general(
            hot, slab_ref[:, step * depth : (step + 1) * depth], NT, preferred_element_type=jnp.float32
        )
        total = part if total is None else total + part
    out_ref[...] = total.astype(out_ref.dtype)


def spread_rows(slab, child_map, targets, tile):
    depth = slab.shape[1] // 8
    count, width = targets.shape[0], slab.shape[0]
    return pl.pallas_call(
        functools.partial(spread_kernel, depth),
        out_shape=jax.ShapeDtypeStruct((count, width), jnp.bfloat16),
        grid=(count // tile,),
        in_specs=[
            pl.BlockSpec((tile, 1), lambda n: (n, 0)),
            pl.BlockSpec((8, 1, depth), lambda n: (0, 0, 0)),
            pl.BlockSpec(slab.shape, lambda n: (0, 0)),
        ],
        out_specs=pl.BlockSpec((tile, width), lambda n: (n, 0)),
        compiler_params=pltpu.CompilerParams(vmem_limit_bytes=VMEM_LIMIT),
        cost_estimate=pl.CostEstimate(
            flops=2 * count * width * slab.shape[1], bytes_accessed=2 * slab.size + 2 * count * width, transcendentals=0
        ),
    )(targets[:, None], child_map.reshape(8, 1, depth), slab)


def place_kernel(target_ref, map_ref, rows_ref, out_ref):
    total = None
    for source in range(map_ref.shape[0]):
        hot = one_hot_tile(target_ref[...], map_ref[source])
        part = lax.dot_general(hot, rows_ref[source], NT, preferred_element_type=jnp.float32)
        total = part if total is None else total + part
    out_ref[...] = total.T.astype(out_ref.dtype)


def place_columns(received, child_map, targets, tile):
    owners, height, depth = received.shape
    count = targets.shape[0]
    return pl.pallas_call(
        place_kernel,
        out_shape=jax.ShapeDtypeStruct((height, count), jnp.bfloat16),
        grid=(count // tile,),
        in_specs=[
            pl.BlockSpec((tile, 1), lambda n: (n, 0)),
            pl.BlockSpec((owners, 1, depth), lambda n: (0, 0, 0)),
            pl.BlockSpec(received.shape, lambda n: (0, 0, 0)),
        ],
        out_specs=pl.BlockSpec((height, tile), lambda n: (0, n)),
        compiler_params=pltpu.CompilerParams(vmem_limit_bytes=VMEM_LIMIT),
        cost_estimate=pl.CostEstimate(
            flops=2 * received.size * count, bytes_accessed=2 * received.size + 2 * height * count, transcendentals=0
        ),
    )(targets[:, None], child_map.reshape(owners, 1, depth), received)


def dot_exact(left, right, dims=(((1,), (0,)), ((), ()))):
    return lax.dot_general(left, right, dims, precision=HIGHEST, preferred_element_type=jnp.float32)


def inverse_kernel(block, pivot_ref, inverse_ref, work_ref, diag_ref, side_ref):
    order = pivot_ref.shape[0]
    work_ref[...] = pivot_ref[...]
    rows = lax.broadcasted_iota(jnp.int32, (order, order), 0)
    cols = lax.broadcasted_iota(jnp.int32, (order, order), 1)
    inverse_ref[...] = jnp.where(rows == cols, 1.0, 0.0)
    small_rows = lax.broadcasted_iota(jnp.int32, (block, block), 0)
    small_cols = lax.broadcasted_iota(jnp.int32, (block, block), 1)
    row_ids = lax.broadcasted_iota(jnp.int32, (block, 1), 0)
    col_ids = lax.broadcasted_iota(jnp.int32, (1, block), 1)
    for first in range(0, order, block):
        last = first + block
        diag_ref[...] = work_ref[first:last, first:last]
        side_ref[...] = jnp.where(small_rows == small_cols, 1.0, 0.0)

        def eliminate(step, carry):
            diag = diag_ref[...]
            column = jnp.sum(jnp.where(small_cols == step, diag, 0.0), axis=1, keepdims=True)
            pivot_row = diag_ref[pl.ds(step, 1), :]
            side_row = side_ref[pl.ds(step, 1), :]
            pivot = jnp.sum(jnp.where(col_ids == step, pivot_row, 0.0), axis=1, keepdims=True)
            ratio = jnp.where(row_ids > step, column / pivot, 0.0)
            diag_ref[...] = diag - ratio * pivot_row
            side_ref[...] = side_ref[...] - ratio * side_row
            return carry

        lax.fori_loop(0, block, eliminate, 0)
        pivots = jnp.sum(jnp.where(small_rows == small_cols, diag_ref[...], 0.0), axis=1, keepdims=True)
        small_inverse = side_ref[...] / jnp.sqrt(pivots)
        top_work = dot_exact(small_inverse, work_ref[first:last, :])
        top_side = dot_exact(small_inverse, inverse_ref[first:last, :])
        inverse_ref[first:last, :] = top_side
        if last < order:
            below = dot_exact(work_ref[last:, first:last], small_inverse, NT)
            work_ref[last:, :] = work_ref[last:, :] - dot_exact(below, top_work)
            inverse_ref[last:, :] = inverse_ref[last:, :] - dot_exact(below, top_side)


def inverse_factor(pivot):
    order, block = pivot.shape[0], 128
    return pl.pallas_call(
        functools.partial(inverse_kernel, block),
        out_shape=jax.ShapeDtypeStruct((order, order), jnp.float32),
        in_specs=[pl.BlockSpec(memory_space=pltpu.VMEM)],
        out_specs=pl.BlockSpec(memory_space=pltpu.VMEM),
        scratch_shapes=[
            pltpu.VMEM((order, order), jnp.float32),
            pltpu.VMEM((block, block), jnp.float32),
            pltpu.VMEM((block, block), jnp.float32),
        ],
        compiler_params=pltpu.CompilerParams(vmem_limit_bytes=VMEM_LIMIT),
        cost_estimate=pl.CostEstimate(flops=40_000_000_000, bytes_accessed=8 * order * order, transcendentals=0),
    )(pivot)


def two_parts(value):
    high = value.astype(jnp.bfloat16)
    return high, (value - high.astype(jnp.float32)).astype(jnp.bfloat16)


def update_kernel(front_ref, own_ref, other_ref, factor_ref, columns_ref, *rest):
    out_ref = rest[-1]
    high, low = two_parts(factor_ref[...])
    col_high, col_low = two_parts(columns_ref[...])

    def product(left, right):
        return lax.dot_general(left, right, NT, preferred_element_type=jnp.float32)

    term = product(high, col_high) + (product(high, col_low) + product(low, col_high))
    placed = own_ref[...].astype(jnp.float32) + other_ref[...].astype(jnp.float32)
    out_ref[...] = (front_ref[...] + placed) - term


def update_rows(chunk, front, own, other, factor, columns, result, tile):
    rows, width = own.shape
    depth = factor.shape[1]
    front_spec = pl.BlockSpec((rows, tile), lambda n: (chunk, n))
    tile_spec = pl.BlockSpec((rows, tile), lambda n: (0, n))
    in_specs = [
        front_spec,
        tile_spec,
        tile_spec,
        pl.BlockSpec((rows, depth), lambda n: (0, 0)),
        pl.BlockSpec((tile, depth), lambda n: (n, 0)),
    ]
    operands = [front, own, other, factor, columns]
    aliases = {}
    if result is not None:
        in_specs.append(pl.BlockSpec(memory_space=pl.ANY))
        operands.append(result)
        aliases = {5: 0}
    return pl.pallas_call(
        update_kernel,
        out_shape=jax.ShapeDtypeStruct(front.shape, jnp.float32),
        grid=(width // tile,),
        in_specs=in_specs,
        out_specs=front_spec,
        input_output_aliases=aliases,
        compiler_params=pltpu.CompilerParams(vmem_limit_bytes=VMEM_LIMIT),
        cost_estimate=pl.CostEstimate(
            flops=6 * rows * width * depth, bytes_accessed=12 * rows * width + 4 * width * depth, transcendentals=0
        ),
    )(*operands)


def shards(parent_front, child_block, child_panel, row_map):
    owners = lax.axis_size("grid")
    cube_pos = lax.axis_index("cube")
    grid_pos = lax.axis_index("grid")
    half_index = cube_pos % 2
    other_index = 1 - half_index
    owned_rows = parent_front.shape[0]
    half_cols = parent_front.shape[2]
    chunk_rows = owned_rows // CHUNKS
    front = parent_front.reshape(owned_rows, half_cols)
    own_panel = child_panel[0]
    own_map = lax.dynamic_index_in_dim(row_map, cube_pos, 0, keepdims=False)

    own_cols = front[:, : PW // 2]
    partner_cols = swapped(own_cols, "cube", 0)
    pairs, panel_ids = lax.iota(jnp.int32, PW // 2), lax.iota(jnp.int32, PW)
    own_pick = (2 * pairs[:, None] + half_index == panel_ids[None, :]).astype(jnp.float32)
    other_pick = (2 * pairs[:, None] + other_index == panel_ids[None, :]).astype(jnp.float32)
    front_panel = dot_exact(own_cols, own_pick) + dot_exact(partner_cols, other_pick)

    products = jnp.einsum(
        "ik,jk->ij",
        own_panel,
        lax.all_gather(child_panel, "grid", axis=1, tiled=True)[0],
        preferred_element_type=jnp.float32,
    )
    contrib = (child_block[0].astype(jnp.float32) - products).astype(jnp.bfloat16)

    slots = lax.iota(jnp.int32, owners * chunk_rows)
    slot_rows = slots // chunk_rows * owned_rows + slots % chunk_rows
    spread_tile = min(512, owners * chunk_rows)
    column_tile = 512
    received = []
    for chunk in range(CHUNKS):
        sent = spread_rows(contrib, own_map, slot_rows + chunk * chunk_rows, spread_tile)
        sent = sent.reshape(owners, chunk_rows, contrib.shape[0])
        received.append(lax.all_to_all(sent, "grid", split_axis=0, concat_axis=0, tiled=True))

    half_ids = lax.iota(jnp.int32, half_cols)
    panels, owns, others = [], [], []
    for chunk in range(CHUNKS):
        panel_part = place_columns(received[chunk], own_map, panel_ids, column_tile)
        partner_part = swapped(panel_part, "cube", 0)
        base = front_panel[chunk * chunk_rows : (chunk + 1) * chunk_rows]
        panels.append(base + (panel_part.astype(jnp.float32) + partner_part.astype(jnp.float32)))
        outgoing = place_columns(received[chunk], own_map, 2 * half_ids + other_index, column_tile)
        others.append(swapped(outgoing, "cube", 0))
        owns.append(place_columns(received[chunk], own_map, 2 * half_ids + half_index, column_tile))

    top = jnp.zeros((PW, PW), jnp.float32)
    for chunk in range(CHUNKS):
        if chunk * chunk_rows < PW:
            start = grid_pos * owned_rows + chunk * chunk_rows
            inside = start < PW
            at = jnp.where(inside, start, 0)
            kept = lax.dynamic_slice_in_dim(top, at, chunk_rows, 0)
            top = lax.dynamic_update_slice_in_dim(top, jnp.where(inside, panels[chunk], kept), at, 0)
    pivot_block = lax.psum(top, "grid")
    inverse = inverse_factor(pivot_block)
    half_inverse = dot_exact(own_pick, inverse)

    row_ids = lax.iota(jnp.int32, chunk_rows)
    row_pick = (2 * row_ids[: chunk_rows // 2, None] + half_index == row_ids[None, :]).astype(jnp.float32)
    factors, halves, gathered = [], [], []
    for chunk in range(CHUNKS):
        factors.append(dot_exact(panels[chunk], inverse, NT))
        halves.append(dot_exact(panels[chunk], half_inverse, NT))
        mine = dot_exact(row_pick, factors[chunk])
        gathered.append(lax.all_gather(mine, "grid", axis=0, tiled=False))
    columns = jnp.stack(gathered, axis=1).reshape(half_cols, PW)

    schur = None
    for chunk in range(CHUNKS):
        schur = update_rows(
            chunk, front, owns[chunk], others[chunk], factors[chunk], columns, schur, min(1024, half_cols)
        )
    panel_rows = jnp.concatenate(halves, axis=0)
    return (schur[:, None, :], panel_rows[:, None, :])


def solution(mesh):
    in_specs = (P("grid", "cube", None), P("cube", "grid", None), P("cube", "grid", None), P())
    out_specs = (P("grid", "cube", None), P("grid", "cube", None))
    return jax.shard_map(shards, mesh=mesh, in_specs=in_specs, out_specs=out_specs, check_vma=False)
```

```python
import functools

import jax
import jax.numpy as jnp
from jax import lax
from jax.experimental import pallas as pl
from jax.experimental.pallas import tpu as pltpu
from jax.sharding import PartitionSpec as P

PW = 512
LANES = 128
CHUNKS = 4
HIGHEST = lax.Precision.HIGHEST
NT = (((1,), (1,)), ((), ()))
VMEM_LIMIT = 56 * 1024 * 1024


def swapped(block, axis, distance):
    count = lax.axis_size(axis)
    route = []
    for low in range(count):
        high = low | 1 << distance
        if high != low and high < count:
            route += [(low, high), (high, low)]
    return lax.ppermute(block, axis, route)


def one_hot_tile(targets, sources):
    return jnp.where(targets == sources, 1.0, 0.0).astype(jnp.bfloat16)


def spread_kernel(depth, target_ref, map_ref, slab_ref, *rest):
    out_ref, total = rest[-1], None
    for step in range(map_ref.shape[0]):
        hot = one_hot_tile(target_ref[...], map_ref[step])
        part = lax.dot_general(
            hot, slab_ref[:, step * depth : (step + 1) * depth], NT, preferred_element_type=jnp.float32
        )
        total = part if total is None else total + part
    out_ref[...] = total.astype(out_ref.dtype)


def spread_rows(slab, child_map, targets, tile, after=()):
    depth = slab.shape[1] // 8
    count, width = targets.shape[0], slab.shape[0]
    return pl.pallas_call(
        functools.partial(spread_kernel, depth),
        out_shape=jax.ShapeDtypeStruct((count, width), jnp.bfloat16),
        grid=(count // tile,),
        in_specs=[
            pl.BlockSpec((tile, 1), lambda n: (n, 0)),
            pl.BlockSpec((8, 1, depth), lambda n: (0, 0, 0)),
            pl.BlockSpec(slab.shape, lambda n: (0, 0)),
        ]
        + [pl.BlockSpec(memory_space=pl.ANY)] * len(after),
        out_specs=pl.BlockSpec((tile, width), lambda n: (n, 0)),
        compiler_params=pltpu.CompilerParams(vmem_limit_bytes=VMEM_LIMIT),
        cost_estimate=pl.CostEstimate(
            flops=2 * count * width * slab.shape[1], bytes_accessed=2 * slab.size + 2 * count * width, transcendentals=0
        ),
    )(targets[:, None], child_map.reshape(8, 1, depth), slab, *after)


def place_kernel(target_ref, map_ref, rows_ref, *rest):
    out_ref, total = rest[-1], None
    for source in range(map_ref.shape[0]):
        hot = one_hot_tile(target_ref[...], map_ref[source])
        part = lax.dot_general(hot, rows_ref[source], NT, preferred_element_type=jnp.float32)
        total = part if total is None else total + part
    out_ref[...] = total.T.astype(out_ref.dtype)


def place_columns(received, child_map, targets, tile, after=()):
    owners, height, depth = received.shape
    count = targets.shape[0]
    return pl.pallas_call(
        place_kernel,
        out_shape=jax.ShapeDtypeStruct((height, count), jnp.bfloat16),
        grid=(count // tile,),
        in_specs=[
            pl.BlockSpec((tile, 1), lambda n: (n, 0)),
            pl.BlockSpec((owners, 1, depth), lambda n: (0, 0, 0)),
            pl.BlockSpec(received.shape, lambda n: (0, 0, 0)),
        ]
        + [pl.BlockSpec(memory_space=pl.ANY)] * len(after),
        out_specs=pl.BlockSpec((height, tile), lambda n: (0, n)),
        compiler_params=pltpu.CompilerParams(vmem_limit_bytes=VMEM_LIMIT),
        cost_estimate=pl.CostEstimate(
            flops=2 * received.size * count, bytes_accessed=2 * received.size + 2 * height * count, transcendentals=0
        ),
    )(targets[:, None], child_map.reshape(owners, 1, depth), received, *after)


def dot_exact(left, right, dims=(((1,), (0,)), ((), ()))):
    return lax.dot_general(left, right, dims, precision=HIGHEST, preferred_element_type=jnp.float32)


def inverse_kernel(block, pivot_ref, *rest):
    inverse_ref, work_ref, diag_ref, side_ref = rest[-4:]
    order = pivot_ref.shape[0]
    work_ref[...] = pivot_ref[...]
    rows = lax.broadcasted_iota(jnp.int32, (order, order), 0)
    cols = lax.broadcasted_iota(jnp.int32, (order, order), 1)
    inverse_ref[...] = jnp.where(rows == cols, 1.0, 0.0)
    small_rows = lax.broadcasted_iota(jnp.int32, (block, block), 0)
    small_cols = lax.broadcasted_iota(jnp.int32, (block, block), 1)
    row_ids = lax.broadcasted_iota(jnp.int32, (block, 1), 0)
    col_ids = lax.broadcasted_iota(jnp.int32, (1, block), 1)
    for first in range(0, order, block):
        last = first + block
        diag_ref[...] = work_ref[first:last, first:last]
        side_ref[...] = jnp.where(small_rows == small_cols, 1.0, 0.0)

        def eliminate(step, carry):
            diag = diag_ref[...]
            column = jnp.sum(jnp.where(small_cols == step, diag, 0.0), axis=1, keepdims=True)
            pivot_row = diag_ref[pl.ds(step, 1), :]
            side_row = side_ref[pl.ds(step, 1), :]
            pivot = jnp.sum(jnp.where(col_ids == step, pivot_row, 0.0), axis=1, keepdims=True)
            ratio = jnp.where(row_ids > step, column / pivot, 0.0)
            diag_ref[...] = diag - ratio * pivot_row
            side_ref[...] = side_ref[...] - ratio * side_row
            return carry

        lax.fori_loop(0, block, eliminate, 0)
        pivots = jnp.sum(jnp.where(small_rows == small_cols, diag_ref[...], 0.0), axis=1, keepdims=True)
        small_inverse = side_ref[...] / jnp.sqrt(pivots)
        top_work = dot_exact(small_inverse, work_ref[first:last, :])
        top_side = dot_exact(small_inverse, inverse_ref[first:last, :])
        inverse_ref[first:last, :] = top_side
        if last < order:
            below = dot_exact(work_ref[last:, first:last], small_inverse, NT)
            work_ref[last:, :] = work_ref[last:, :] - dot_exact(below, top_work)
            inverse_ref[last:, :] = inverse_ref[last:, :] - dot_exact(below, top_side)


def inverse_factor(pivot, after):
    order, block = pivot.shape[0], 128
    return pl.pallas_call(
        functools.partial(inverse_kernel, block),
        out_shape=jax.ShapeDtypeStruct((order, order), jnp.float32),
        in_specs=[pl.BlockSpec(memory_space=pltpu.VMEM)] + [pl.BlockSpec(memory_space=pl.ANY)] * len(after),
        out_specs=pl.BlockSpec(memory_space=pltpu.VMEM),
        scratch_shapes=[
            pltpu.VMEM((order, order), jnp.float32),
            pltpu.VMEM((block, block), jnp.float32),
            pltpu.VMEM((block, block), jnp.float32),
        ],
        compiler_params=pltpu.CompilerParams(vmem_limit_bytes=VMEM_LIMIT),
        cost_estimate=pl.CostEstimate(flops=40_000_000_000, bytes_accessed=8 * order * order, transcendentals=0),
    )(pivot, *after)


def two_parts(value):
    high = value.astype(jnp.bfloat16)
    return high, (value - high.astype(jnp.float32)).astype(jnp.bfloat16)


def update_kernel(front_ref, own_ref, other_ref, factor_ref, columns_ref, *rest):
    out_ref = rest[-1]
    high, low = two_parts(factor_ref[...])
    col_high, col_low = two_parts(columns_ref[...])

    def product(left, right):
        return lax.dot_general(left, right, NT, preferred_element_type=jnp.float32)

    term = product(high, col_high) + (product(high, col_low) + product(low, col_high))
    placed = own_ref[...].astype(jnp.float32) + other_ref[...].astype(jnp.float32)
    value = (front_ref[...] + placed) - term
    for part in range(out_ref.shape[1]):
        out_ref[:, part, :] = value[:, part * LANES : (part + 1) * LANES]


def update_rows(chunk, front, own, other, factor, columns, result, tile):
    rows, width = own.shape
    depth = factor.shape[1]
    front_spec = pl.BlockSpec((rows, tile), lambda n: (chunk, n))
    tile_spec = pl.BlockSpec((rows, tile), lambda n: (0, n))
    in_specs = [
        front_spec,
        tile_spec,
        tile_spec,
        pl.BlockSpec((rows, depth), lambda n: (0, 0)),
        pl.BlockSpec((tile, depth), lambda n: (n, 0)),
    ]
    operands = [front, own, other, factor, columns]
    aliases = {}
    if result is not None:
        in_specs.append(pl.BlockSpec(memory_space=pl.ANY))
        operands.append(result)
        aliases = {5: 0}
    return pl.pallas_call(
        update_kernel,
        out_shape=jax.ShapeDtypeStruct((front.shape[0], width // LANES, LANES), jnp.float32),
        grid=(width // tile,),
        in_specs=in_specs,
        out_specs=pl.BlockSpec((rows, tile // LANES, LANES), lambda n: (chunk, n, 0)),
        input_output_aliases=aliases,
        compiler_params=pltpu.CompilerParams(vmem_limit_bytes=VMEM_LIMIT),
        cost_estimate=pl.CostEstimate(
            flops=6 * rows * width * depth, bytes_accessed=12 * rows * width + 4 * width * depth, transcendentals=0
        ),
    )(*operands)


def shards(parent_front, child_block, child_panel, row_map):
    owners = lax.axis_size("grid")
    cube_pos = lax.axis_index("cube")
    grid_pos = lax.axis_index("grid")
    half_index = cube_pos % 2
    other_index = 1 - half_index
    owned_rows = parent_front.shape[0]
    half_cols = parent_front.shape[2]
    chunk_rows = owned_rows // CHUNKS
    front = parent_front.reshape(owned_rows, half_cols)
    own_panel = child_panel[0]
    own_map = lax.dynamic_index_in_dim(row_map, cube_pos, 0, keepdims=False)

    own_cols = front[:, : PW // 2]
    partner_cols = swapped(own_cols, "cube", 0)
    pairs, panel_ids = lax.iota(jnp.int32, PW // 2), lax.iota(jnp.int32, PW)
    own_pick = (2 * pairs[:, None] + half_index == panel_ids[None, :]).astype(jnp.float32)
    other_pick = (2 * pairs[:, None] + other_index == panel_ids[None, :]).astype(jnp.float32)
    front_panel = dot_exact(own_cols, own_pick) + dot_exact(partner_cols, other_pick)

    products = jnp.einsum(
        "ik,jk->ij",
        own_panel,
        lax.all_gather(child_panel, "grid", axis=1, tiled=True)[0],
        preferred_element_type=jnp.float32,
    )
    contrib = (child_block[0].astype(jnp.float32) - products).astype(jnp.bfloat16)

    slots = lax.iota(jnp.int32, owners * chunk_rows)
    slot_rows = slots // chunk_rows * owned_rows + slots % chunk_rows
    spread_tile = min(512, owners * chunk_rows)
    column_tile = 512
    half_ids = lax.iota(jnp.int32, half_cols)
    base_rows = [front_panel[c * chunk_rows : (c + 1) * chunk_rows] for c in range(CHUNKS)]
    pivot_chunks = [chunk for chunk in range(CHUNKS) if chunk * chunk_rows < PW]
    inverse_chunk = max(1, pivot_chunks[-1])
    early_chunks = range(CHUNKS // 2)
    sent, received, panels = {}, {}, {}
    owns, others, inverse = {}, {}, None

    def spread(chunk, after):
        sent[chunk] = spread_rows(contrib, own_map, slot_rows + chunk * chunk_rows, spread_tile, after)
        blocks = sent[chunk].reshape(owners, chunk_rows, contrib.shape[0])
        received[chunk] = lax.all_to_all(blocks, "grid", split_axis=0, concat_axis=0, tiled=True)

    def place(chunk, targets, after):
        return place_columns(received[chunk], own_map, targets, column_tile, after)

    row_ids = lax.iota(jnp.int32, chunk_rows)
    row_pick = (2 * row_ids[: chunk_rows // 2, None] + half_index == row_ids[None, :]).astype(jnp.float32)

    def parity_rows(panel, inverse):
        return dot_exact(dot_exact(row_pick, panel), inverse, NT)

    def inverse_of_pivot(after):
        top = jnp.zeros((PW, PW), jnp.float32)
        for chunk in pivot_chunks:
            start = grid_pos * owned_rows + chunk * chunk_rows
            inside = start < PW
            at = jnp.where(inside, start, 0)
            kept = lax.dynamic_slice_in_dim(top, at, chunk_rows, 0)
            top = lax.dynamic_update_slice_in_dim(top, jnp.where(inside, panels[chunk], kept), at, 0)
        return inverse_factor(lax.psum(top, "grid"), after)

    spread(0, ())
    spread(1, (sent[0],))
    last, ready = sent[1], ()
    for chunk in range(CHUNKS):
        arrived = (others[chunk - 1],) if chunk else ()
        wanted = arrived if chunk == CHUNKS - 1 else ready
        panel_part = place(chunk, panel_ids, (last,) + wanted)
        partner_part = swapped(panel_part, "cube", 0)
        panels[chunk] = base_rows[chunk] + (panel_part.astype(jnp.float32) + partner_part.astype(jnp.float32))
        outgoing = place(chunk, 2 * half_ids + other_index, (panel_part,))
        others[chunk] = swapped(outgoing, "cube", 0)
        last = outgoing
        if chunk + 2 < CHUNKS:
            owns[chunk] = place(chunk, 2 * half_ids + half_index, (outgoing,) + arrived)
            spread(chunk + 2, (owns[chunk],))
            last = sent[chunk + 2]
        if chunk == inverse_chunk:
            inverse = last = inverse_of_pivot((last,) + arrived)
            early_rows = jnp.stack([parity_rows(panels[c], inverse) for c in early_chunks])
            early = lax.all_gather(early_rows, "grid", axis=0, tiled=False)
            ready = (early_rows,)
        elif chunk == CHUNKS - 2:
            last = owns[chunk] = place(chunk, 2 * half_ids + half_index, (outgoing,) + arrived)
    owns[CHUNKS - 1] = place(CHUNKS - 1, 2 * half_ids + half_index, (outgoing,))
    half_inverse = dot_exact(own_pick, inverse)

    factors, halves = [], []
    for chunk in range(CHUNKS):
        factors.append(dot_exact(panels[chunk], inverse, NT))
        halves.append(dot_exact(panels[chunk], half_inverse, NT))
    late_rows = jnp.stack([parity_rows(panels[c], inverse) for c in range(CHUNKS // 2, CHUNKS)])
    late = lax.all_gather(late_rows, "grid", axis=0, tiled=False)
    columns = jnp.concatenate([early, late], axis=1).reshape(half_cols, PW)

    schur = None
    for chunk in range(CHUNKS):
        schur = update_rows(
            chunk, front, owns[chunk], others[chunk], factors[chunk], columns, schur, min(1024, half_cols)
        )
    panel_rows = jnp.concatenate(halves, axis=0)
    return (schur.reshape(parent_front.shape), panel_rows[:, None, :])


def solution(mesh):
    in_specs = (P("grid", "cube", None), P("cube", "grid", None), P("cube", "grid", None), P())
    out_specs = (P("grid", "cube", None), P("grid", "cube", None))
    return jax.shard_map(shards, mesh=mesh, in_specs=in_specs, out_specs=out_specs, check_vma=False)
```
